128 devices in a mesh: group: 4 (over y), dev: 32 (over x, z, core).
Axes of the slice: x: 4, y: 4, z: 4, core: 2. Of those that a mesh axis runs over, the one named last changes fastest.
Arguments:
- a_tiles: bfloat16 [4096, 2, 2, 256, 256], P(('group', 'dev')), may hold values from -4 to 4
- scaling: float32 [4096, 2, 256], P(('group', 'dev')), may hold values from 0.2 to 5
- dest_owner: int32 [4096, 1], P(('group', 'dev')), may hold values from 0 to 31; in each aligned block of 32 rows (0 to 31, 32 to 63, ...) at most 2 rows name the same one
- dest_slot: int32 [4096], P(('group', 'dev')), may hold values from 0 to 15
- panel: bfloat16 [8192, 512], P('dev', 'group'), may hold values from -3.59375 to 3.59375
- front_tiles: int32 [512, 2], P(('group', 'dev')), may hold values from 0 to 31
Outputs:
- schur: float32 [512, 256, 256], P(('group', 'dev'))
The draws below stay inside these ranges and needn't reach their ends.
Inputs may be any that keep to these rules, and one draw needn't show every extreme that they name: `dest_owner`: among the 32 contributions of one device, no owner is named more than 2 times, a bound that some block reaches.
All inputs are finite; a program needn't handle non-finite values.
Results may differ from the reference program's by a relative error of at most 0.0031.
Values may be sent and summed in bfloat16 or wider, within the bound.
No kernel may reach another device: no remote copies, remote signals or barrier semaphores. Data moves between devices by JAX's collectives and lax.ppermute only.
A program may use at most 128 MiB of HBM per device.

```python
import math
import jax
import jax.numpy as jnp
import numpy as np
from jax import lax

B = 256
K = 2
C_DEV = 32
SQ = 4
PW = 512
CAP = 2
CONTRIBS = 4096
S_DEV = 16
S_TILES = 512
PANEL_TILES = 32
PANEL_ROWS = 8192
N_DEV = 32


def touch_ends(drawn, stream_key, low, largest):
    shape = drawn.shape
    place = [jax.random.randint(jax.random.fold_in(stream_key, axis), (), 0, shape[axis]) for axis in range(len(shape))]
    drawn = drawn.at[tuple(place)].set(low)
    longest = shape.index(max(shape))
    place[longest] = (place[longest] + 1) % shape[longest]
    return drawn.at[tuple(place)].set(largest)


def block_levels(key, shape, cuts, smallest, top_value):
    factor_of = 1.0
    for axis_at, shards_of in cuts:
        heights = jax.random.uniform(jax.random.fold_in(jax.random.fold_in(key, 6), axis_at), (shards_of,), jnp.float32, smallest / len(cuts), top_value / len(cuts))
        factor_of = factor_of * jnp.repeat(jnp.exp(heights), shape[axis_at] // shards_of).reshape((-1,) + (1,) * (len(shape) - 1 - axis_at))
    return factor_of


def deal_out(rng, own, number, rows, count, top, reach, slope):
    sequence = jax.random.permutation(rng, count)
    heavy_load, ordinary = portions_of(count, rows * top, reach, slope, True), portions_of(count, rows * top, reach, slope, False)
    places = jnp.arange(count)

    def named(lengths, turn):
        used = int((lengths > 0).sum())
        fixed = max(1, used // 4)
        moved = fixed + (places - fixed + turn * (used - fixed)) % max(1, count - fixed)
        return jnp.zeros((count,), jnp.int32).at[sequence[jnp.where(places < fixed, places, moved)]].set(jnp.asarray(lengths, jnp.int32))

    lengths = jnp.where(number % 4 == 0, named(heavy_load, number // 4), named(ordinary, number - number // 4 - 1))
    mixed = jax.random.permutation(jax.random.fold_in(own, 3), count)
    source_of, taker = mixed[0:count // 2 * 2:2], mixed[1:count // 2 * 2:2]
    margin = jnp.minimum(lengths[source_of] - 1, reach - lengths[taker]) // 2
    margin = jnp.where((source_of == sequence[0]) | (taker == sequence[0]) | (lengths[taker] == 0), 0, jnp.maximum(margin, 0))
    moved = jax.random.randint(jax.random.fold_in(own, 4), (count // 2,), 0, 1 << 20) % (margin + 1)
    lengths = lengths.at[source_of].add(-moved).at[taker].add(moved)
    items = jnp.searchsorted(jnp.cumsum(lengths), jnp.arange(rows * top), side="right").astype(jnp.int32)
    table = items.reshape(top, rows).T
    table = table[jax.random.permutation(jax.random.fold_in(own, 1), rows)]
    turn = jax.random.randint(jax.random.fold_in(own, 2), (rows, 1), 0, top)
    return jnp.take_along_axis(table, (jnp.arange(top)[None, :] + turn) % top, axis=1)


def portions_of(number_of, total, bound, lean, full):
    weights = [(1 << 20) // math.isqrt(standing ** lean) + 1 for standing in range(1, number_of + 1)]
    largest = bound if full else min(bound, max(-(-total // number_of), total * weights[0] // sum(weights)))
    least = 1 if total - largest >= number_of - 1 else 0
    holding, spare = [largest] + [least] * (number_of - 1), total - largest - least * (number_of - 1)
    while spare > 0:
        free = [i for i in range(1, number_of) if holding[i] < largest] or [i for i in range(1, number_of) if holding[i] < bound]
        whole, left = sum([weights[i] for i in free]), spare
        for i in free:
            extra = min(bound - holding[i], max(1, left * weights[i] // whole), spare)
            holding[i] = holding[i] + extra
            spare = spare - extra
    return np.array(holding)


def normal_values(own_key, dims, scale, most, cuts=(), held_as=jnp.bfloat16):
    drawn = jax.random.normal(own_key, dims, jnp.float32) * scale
    if len(cuts) > 0:
        drawn = block_levels(own_key, dims, cuts, -0.22, 0.18) * drawn
    return jnp.clip(drawn, min=-most, max=most).astype(held_as)


def setup_inputs(seed: int = 0) -> dict:
    streams_of = jax.random.split(jax.random.key(seed), 7)
    a_tiles = normal_values(streams_of[0], (CONTRIBS, K, 2, B, B), 0.25, 4.0, ((0, 128),))
    scaling = jnp.clip(jnp.exp(math.log(5.0) - 3.218876 * jax.random.uniform(streams_of[1], (CONTRIBS, K, B), jnp.float32) ** block_levels(streams_of[1], (CONTRIBS, K, B), ((0, 128),), -0.2, 0.2)), 0.2, 5.0)
    dest_owner_keys = jax.random.split(jax.random.fold_in(streams_of[2], 1), CONTRIBS // C_DEV)
    dest_owner_turns = jax.random.permutation(jax.random.fold_in(streams_of[2], 3), CONTRIBS // C_DEV)
    dest_owner = jax.vmap(lambda own, number: deal_out(jax.random.fold_in(streams_of[2], 2), own, number, C_DEV, N_DEV, 1, CAP, 2))(dest_owner_keys, dest_owner_turns).reshape((CONTRIBS, 1))
    dest_slot = touch_ends(jax.random.randint(streams_of[3], (CONTRIBS,), 0, S_DEV), jax.random.fold_in(streams_of[3], 1), 0, S_DEV - 1).astype(jnp.int32)
    panel = normal_values(streams_of[4], (PANEL_ROWS, PW), 0.6, 3.59375, ((0, 32), (1, 4)))
    front_tiles = touch_ends(jax.random.randint(streams_of[5], (S_TILES, 2), 0, PANEL_TILES), jax.random.fold_in(streams_of[5], 1), 0, PANEL_TILES - 1).astype(jnp.int32)
    return {"a_tiles": a_tiles, "scaling": scaling, "dest_owner": dest_owner, "dest_slot": dest_slot, "panel": panel, "front_tiles": front_tiles}


def form_one(args):
    tiles, column_scale = args
    scaled = (tiles[:, 0].astype(jnp.float32) * column_scale[:, None, :]).astype(jnp.bfloat16)
    scaled = lax.optimization_barrier(scaled)
    summed = jnp.einsum("kij,kmj->im", scaled.astype(jnp.float32), tiles[:, 1].astype(jnp.float32))
    return summed.astype(jnp.bfloat16)


def reference(a_tiles, scaling, dest_owner, dest_slot, panel, front_tiles):
    products = lax.map(form_one, (a_tiles, scaling))
    products = lax.optimization_barrier(products)
    owner_ids = dest_owner[:, 0].astype(jnp.int32)
    slot_ids = dest_slot.astype(jnp.int32)
    target = (slot_ids // SQ) * (N_DEV * SQ) + owner_ids * SQ + slot_ids % SQ
    assembled = jnp.zeros((S_TILES, B, B), jnp.float32).at[target].add(products.astype(jnp.float32))
    pieces = panel.reshape(PANEL_TILES, B, PW)
    left_tiles = pieces[front_tiles[:, 0]].astype(jnp.float32)
    right_tiles = pieces[front_tiles[:, 1]].astype(jnp.float32)
    update = jnp.einsum("sbp,scp->sbc", left_tiles, right_tiles)
    return assembled - update
```

```python
import jax
import jax.numpy as jnp
from jax import lax
from jax.sharding import PartitionSpec as P

AXES = ("group", "dev")


def per_device(a_tiles, scaling, dest_owner, dest_slot, panel, front_tiles):
    contribs, _, _, tile, _ = a_tiles.shape
    n_dev = lax.axis_size("dev")
    n_group = lax.axis_size("group")
    n_all = n_dev * n_group
    held = front_tiles.shape[0]
    chunk = tile * tile // n_all

    panel_all = lax.all_gather(panel, AXES, axis=0, tiled=True)

    target = (dest_slot // held) * (n_dev * held) + dest_owner[:, 0] * held + dest_slot % held
    targets = lax.all_to_all(
        jnp.broadcast_to(target[None, :], (n_all, contribs)), AXES, split_axis=0, concat_axis=0, tiled=True
    ).reshape(-1)

    scaled = (a_tiles[:, :, 0].astype(jnp.float32) * scaling[:, :, None, :]).astype(jnp.bfloat16)
    products = jnp.einsum(
        "ckij,ckmj->cim", scaled, a_tiles[:, :, 1], preferred_element_type=jnp.float32
    ).astype(jnp.bfloat16)
    outgoing = products.reshape(contribs, n_all, chunk).transpose(1, 0, 2)
    arrived = lax.all_to_all(outgoing, AXES, split_axis=0, concat_axis=0, tiled=True)

    n_tiles = n_all * held
    picking = (targets[None, :] == jnp.arange(n_tiles, dtype=jnp.int32)[:, None]).astype(jnp.bfloat16)
    sums = jnp.dot(picking, arrived.reshape(n_all * contribs, chunk), preferred_element_type=jnp.float32)
    final = lax.all_to_all(
        sums.astype(jnp.bfloat16).reshape(n_all, held, chunk), AXES, split_axis=0, concat_axis=0, tiled=True
    )
    assembled = final.transpose(1, 0, 2).reshape(held, tile, tile).astype(jnp.float32)

    pieces = panel_all.reshape(n_group, n_dev, tile, -1)
    left = jnp.take(pieces, front_tiles[:, 0], axis=1)
    right = jnp.take(pieces, front_tiles[:, 1], axis=1)
    update = jnp.einsum("gsbp,gscp->sbc", left, right, preferred_element_type=jnp.float32)
    return assembled - update


def solution(mesh):
    in_specs = (
        P(AXES, None, None, None, None),
        P(AXES, None, None),
        P(AXES, None),
        P(AXES),
        P("dev", "group"),
        P(AXES, None),
    )
    out_specs = P(AXES, None, None)
    return jax.shard_map(
        per_device, mesh=mesh, in_specs=in_specs, out_specs=out_specs, check_vma=False
    )
```

```python
import functools
import jax
import jax.numpy as jnp
from jax import lax
from jax.experimental import pallas as pl
from jax.experimental.pallas import tpu as pltpu
from jax.sharding import PartitionSpec as P

AXES = ("group", "dev")
LANES = 128
BATCH = 16
VMEM = pltpu.CompilerParams(vmem_limit_bytes=48 << 20)


def exchange(x):
    return lax.all_to_all(x, AXES, split_axis=0, concat_axis=0, tiled=True)


def swap_matrix(per):
    cols = LANES // per
    width = per * LANES
    source = lax.broadcasted_iota(jnp.int32, (width, width), 0)
    dest = lax.broadcasted_iota(jnp.int32, (width, width), 1)
    swapped = (dest // cols % per) * LANES + dest // LANES * cols + dest % cols
    return (source == swapped).astype(jnp.bfloat16)


def early_kernel(n_down, n_across, owner_ref, slot_ref, front_ref, panel_ref, out_ref):
    tile, depth = panel_ref.shape
    rows, cols = tile // n_down, tile // n_across
    count = owner_ref.shape[0]
    lane = lax.broadcasted_iota(jnp.int32, (16, depth), 1)
    numbers = jnp.zeros((16, depth), jnp.int32)
    held = front_ref.shape[1]
    for c in range(count):
        numbers = jnp.where(lane == c, owner_ref[c], numbers)
        numbers = jnp.where(lane == count + c, slot_ref[c], numbers)
    for s in range(held):
        for side in range(2):
            numbers = jnp.where(lane == 2 * count + side * held + s, front_ref[side, s], numbers)
    numbers = numbers.astype(jnp.float32).astype(jnp.bfloat16)
    for i in range(n_down):
        left = panel_ref[i * rows:(i + 1) * rows, :]
        for j in range(n_across):
            out_ref[i * n_across + j, 0:rows, :] = left
            out_ref[i * n_across + j, rows:rows + cols, :] = panel_ref[j * cols:(j + 1) * cols, :]
            out_ref[i * n_across + j, rows + cols:rows + cols + 16, :] = numbers


def early_blocks(owner, slot, front_tiles, panel, n_down, n_across):
    tile, depth = panel.shape
    height = tile // n_down + tile // n_across + 16
    smem = pl.BlockSpec(memory_space=pltpu.SMEM)
    vmem = pl.BlockSpec(memory_space=pltpu.VMEM)
    return pl.pallas_call(
        functools.partial(early_kernel, n_down, n_across),
        in_specs=[smem, smem, smem, vmem],
        out_specs=vmem,
        out_shape=jax.ShapeDtypeStruct((n_down * n_across, height, depth), jnp.bfloat16),
        compiler_params=VMEM,
    )(owner, slot, front_tiles.T, panel)


def products_kernel(n_down, n_across, a_ref, scale_ref, swap_ref, out_ref, held_ref):
    count, blocks, _, tile, _ = a_ref.shape
    rows, cols = tile // n_down, tile // n_across
    per = LANES // cols
    quads = rows // per
    sides = tile // LANES
    step = pl.program_id(1)
    for u in range(count):
        total = None
        for k in range(blocks):
            scaled = (a_ref[u, k, 0].astype(jnp.float32) * scale_ref[u, k][None, :]).astype(jnp.bfloat16)
            part = lax.dot_general(
                scaled, a_ref[u, k, 1], (((1,), (1,)), ((), ())), preferred_element_type=jnp.float32
            )
            total = part if total is None else total + part
        for h in range(sides):
            held_ref[h, pl.ds(step * count + u, tile, stride=BATCH), :] = total[:, h * LANES:(h + 1) * LANES]

    @pl.when(step == pl.num_programs(1) - 1)
    def _():
        together = 4

        @pl.loop(0, n_down // together)
        def _(block):
            at = [(d, q, h) for d in range(together) for q in range(quads) for h in range(sides)]
            parts = []
            for d, q, h in at:
                row = ((block * together + d) * rows + q * per) * BATCH
                parts.append(jnp.concatenate([
                    held_ref[h, pl.ds(pl.multiple_of(row + r * BATCH, BATCH), BATCH), :].astype(jnp.bfloat16)
                    for r in range(per)
                ], axis=1))
            swapped = jnp.dot(
                jnp.concatenate(parts, axis=0), swap_ref[...], preferred_element_type=jnp.float32
            ).astype(jnp.bfloat16)
            for n, (d, q, h) in enumerate(at):
                for j in range(per):
                    out_ref[(block * together + d) * n_across + h * per + j, :, q * LANES:(q + 1) * LANES] = (
                        swapped[n * BATCH:(n + 1) * BATCH, j * LANES:(j + 1) * LANES]
                    )


def form_products(a_tiles, scaling, swap, n_down, n_across):
    contribs, blocks, _, tile, _ = a_tiles.shape
    n_all = n_down * n_across
    chunk = tile * tile // n_all
    count = 8
    steps = BATCH // count
    return pl.pallas_call(
        functools.partial(products_kernel, n_down, n_across),
        grid=(contribs // BATCH, steps),
        in_specs=[
            pl.BlockSpec((count, blocks, 2, tile, tile), lambda g, s: (g * steps + s, 0, 0, 0, 0)),
            pl.BlockSpec((count, blocks, tile), lambda g, s: (g * steps + s, 0, 0)),
            pl.BlockSpec(swap.shape, lambda g, s: (0, 0)),
        ],
        out_specs=pl.BlockSpec((n_all, BATCH, chunk), lambda g, s: (0, g, 0)),
        out_shape=jax.ShapeDtypeStruct((n_all, contribs, chunk), jnp.bfloat16),
        scratch_shapes=[pltpu.VMEM((tile // LANES, tile * BATCH, LANES), jnp.float32)],
        compiler_params=VMEM,
    )(a_tiles, scaling, swap)


def sum_kernel(x_ref, target_ref, update_ref, out_ref, total_ref, spread_ref):
    step = pl.program_id(0)
    n_tiles, chunk = total_ref.shape
    number = lax.broadcasted_iota(jnp.int32, (n_tiles, x_ref.shape[0]), 0)
    picking = (number == target_ref[...]).astype(jnp.float32).astype(jnp.bfloat16)
    part = jnp.dot(picking, x_ref[...], preferred_element_type=jnp.float32)

    @pl.when(step == 0)
    def _():
        total_ref[...] = part - update_ref[...]

    @pl.when(step > 0)
    def _():
        total_ref[...] += part

    @pl.when(step == pl.num_programs(0) - 1)
    def _():
        pieces = chunk // LANES
        for q in range(pieces):
            spread_ref[pl.ds(q, n_tiles, stride=pieces), :] = total_ref[:, q * LANES:(q + 1) * LANES]
        out_ref[...] = spread_ref[...].astype(jnp.bfloat16)


def sum_by_target(x, target, update):
    contribs, chunk = x.shape
    n_tiles = update.shape[0]
    block = 1024
    return pl.pallas_call(
        sum_kernel,
        grid=(contribs // block,),
        in_specs=[
            pl.BlockSpec((block, chunk), lambda s: (s, 0)),
            pl.BlockSpec((1, block), lambda s: (0, s)),
            pl.BlockSpec((n_tiles, chunk), lambda s: (0, 0)),
        ],
        out_specs=pl.BlockSpec((n_tiles * chunk // LANES, LANES), lambda s: (0, 0)),
        out_shape=jax.ShapeDtypeStruct((n_tiles * chunk // LANES, LANES), jnp.bfloat16),
        scratch_shapes=[
            pltpu.VMEM((n_tiles, chunk), jnp.float32),
            pltpu.VMEM((n_tiles * chunk // LANES, LANES), jnp.float32),
        ],
        compiler_params=VMEM,
    )(x, target.reshape(1, -1), update)


def final_kernel(n_down, n_across, x_ref, swap_ref, out_ref, spread_ref):
    held, tile, _ = out_ref.shape
    rows, cols = tile // n_down, tile // n_across
    per = LANES // cols
    quads = rows // per
    sides = tile // LANES
    at = [(i, h) for i in range(n_down) for h in range(sides)]
    parts = []
    for i, h in at:
        first = i * n_across + h * per
        parts.append(jnp.concatenate([x_ref[first + j] for j in range(per)], axis=1))
    swapped = jnp.dot(jnp.concatenate(parts, axis=0), swap_ref[...], preferred_element_type=jnp.float32)
    for n, (i, h) in enumerate(at):
        for r in range(per):
            for s in range(held):
                top = n * held * quads + s * quads
                spread_ref[h, pl.ds(s * tile + i * rows + r, quads, stride=per), :] = (
                    swapped[top:top + quads, r * LANES:(r + 1) * LANES]
                )
    for s in range(held):
        for h in range(sides):
            out_ref[s, :, h * LANES:(h + 1) * LANES] = spread_ref[h, s * tile:(s + 1) * tile, :]


def final_tiles(x, swap, tile, held, n_down, n_across):
    vmem = pl.BlockSpec(memory_space=pltpu.VMEM)
    return pl.pallas_call(
        functools.partial(final_kernel, n_down, n_across),
        in_specs=[vmem, vmem],
        out_specs=vmem,
        out_shape=jax.ShapeDtypeStruct((held, tile, tile), jnp.float32),
        scratch_shapes=[pltpu.VMEM((tile // LANES, held * tile, LANES), jnp.float32)],
        compiler_params=VMEM,
    )(x, swap)


def per_device(a_tiles, scaling, dest_owner, dest_slot, panel, front_tiles):
    contribs, _, _, tile, _ = a_tiles.shape
    n_dev = lax.axis_size("dev")
    n_group = lax.axis_size("group")
    n_all = n_dev * n_group
    held = front_tiles.shape[0]
    n_tiles = n_all * held
    n_across = 8
    n_down = n_all // n_across
    rows, cols = tile // n_down, tile // n_across
    chunk = rows * cols
    depth = panel.shape[1]
    swap = swap_matrix(LANES // cols)

    early = exchange(early_blocks(dest_owner[:, 0], dest_slot, front_tiles, panel, n_down, n_across))
    arrived = exchange(form_products(a_tiles, scaling, swap, n_down, n_across))

    numbers = early[:, rows + cols].astype(jnp.int32)
    owner, slot = numbers[:, :contribs].reshape(-1), numbers[:, contribs:2 * contribs].reshape(-1)
    target = (slot // held) * (n_dev * held) + owner * held + slot % held
    first = 2 * contribs
    row_piece = numbers[:, first:first + held].reshape(-1)
    col_piece = numbers[:, first + held:first + 2 * held].reshape(-1)

    early = early.reshape(n_group, n_dev, -1, depth)
    grid = jnp.einsum(
        "glrp,gsmp->lsrm", early[:, :, :rows], early[:, :, rows:rows + cols], preferred_element_type=jnp.float32
    ).reshape(n_dev * n_dev, chunk)
    update = jnp.take(grid, row_piece * n_dev + col_piece, axis=0, mode="clip")

    sums = sum_by_target(arrived.reshape(n_all * contribs, chunk), target, update)
    final = exchange(sums.reshape(n_all, held * chunk // LANES, LANES))
    return final_tiles(final, swap, tile, held, n_down, n_across)


def solution(mesh):
    in_specs = (
        P(AXES, None, None, None, None),
        P(AXES, None, None),
        P(AXES, None),
        P(AXES),
        P("dev", "group"),
        P(AXES, None),
    )
    out_specs = P(AXES, None, None)
    return jax.shard_map(
        per_device, mesh=mesh, in_specs=in_specs, out_specs=out_specs, check_vma=False
    )
```

```python
import functools
import jax
import jax.numpy as jnp
from jax import lax
from jax.experimental import pallas as pl
from jax.experimental.pallas import tpu as pltpu
from jax.sharding import PartitionSpec as P

AXES = ("group", "chip", "core")
PLANE = ("group", "chip")
LANES = 128
BATCH = 16
VMEM = pltpu.CompilerParams(vmem_limit_bytes=48 << 20)


def exchange(x, axes):
    return lax.all_to_all(x, axes, split_axis=0, concat_axis=0, tiled=True)


def device_of(i, j, n_across):
    return (i // 2) * (2 * n_across) + 2 * j + i % 2


def swap_matrix(per):
    cols = LANES // per
    width = per * LANES
    source = lax.broadcasted_iota(jnp.int32, (width, width), 0)
    dest = lax.broadcasted_iota(jnp.int32, (width, width), 1)
    swapped = (dest // cols % per) * LANES + dest // LANES * cols + dest % cols
    return (source == swapped).astype(jnp.bfloat16)


def early_kernel(n_down, n_across, owner_hbm, slot_hbm, front_hbm, panel_hbm, out_ref,
                 owner_ref, slot_ref, front_ref, panel_ref, sem_ref):
    pairs = [(owner_hbm, owner_ref), (slot_hbm, slot_ref), (front_hbm, front_ref), (panel_hbm, panel_ref)]
    copies = [pltpu.make_async_copy(a, b, sem_ref.at[n]) for n, (a, b) in enumerate(pairs)]
    for copy in copies:
        copy.start()
    for copy in copies:
        copy.wait()
    tile, depth = panel_ref.shape
    rows = tile // n_down
    count = owner_ref.shape[0]
    held = front_ref.shape[1]
    lane = lax.broadcasted_iota(jnp.int32, (8, depth), 1)
    numbers = jnp.zeros((8, depth), jnp.int32)
    for c in range(count):
        numbers = jnp.where(lane == c, owner_ref[c], numbers)
        numbers = jnp.where(lane == count + c, slot_ref[c], numbers)
    for s in range(held):
        for side in range(2):
            numbers = jnp.where(lane == 2 * count + side * held + s, front_ref[side, s], numbers)
    numbers = numbers.astype(jnp.float32).astype(jnp.bfloat16)
    cols = tile // n_across
    for a in range(n_down // 2):
        for j in range(n_across):
            chip = a * n_across + j
            out_ref[chip, 0:2 * rows, :] = panel_ref[2 * a * rows:2 * (a + 1) * rows, :]
            out_ref[chip, 2 * rows:2 * rows + cols, :] = panel_ref[j * cols:(j + 1) * cols, :]
            out_ref[chip, 2 * rows + cols:2 * rows + cols + 8, :] = numbers


def early_blocks(owner, slot, front_tiles, panel, n_down, n_across):
    tile, depth = panel.shape
    height = 2 * (tile // n_down) + tile // n_across + 8
    front = front_tiles.T
    hbm = pl.BlockSpec(memory_space=pltpu.HBM)
    return pl.pallas_call(
        functools.partial(early_kernel, n_down, n_across),
        in_specs=[hbm] * 4,
        out_specs=pl.BlockSpec(memory_space=pltpu.VMEM),
        out_shape=jax.ShapeDtypeStruct((n_down * n_across // 2, height, depth), jnp.bfloat16),
        scratch_shapes=[
            pltpu.SMEM(owner.shape, owner.dtype),
            pltpu.SMEM(slot.shape, slot.dtype),
            pltpu.SMEM(front.shape, front.dtype),
            pltpu.VMEM(panel.shape, panel.dtype),
            pltpu.SemaphoreType.DMA((4,)),
        ],
        compiler_params=pltpu.CompilerParams(vmem_limit_bytes=64 << 20),
    )(owner, slot, front, panel)


def products_kernel(n_down, n_across, a_ref, scale_ref, swap_ref, out_ref, held_ref):
    count, blocks, _, tile, _ = a_ref.shape
    rows, cols = tile // n_down, tile // n_across
    per = LANES // cols
    quads = rows // per
    sides = tile // LANES
    step = pl.program_id(1)
    for u in range(count):
        total = None
        for k in range(blocks):
            scaled = (a_ref[u, k, 0].astype(jnp.float32) * scale_ref[u, k][None, :]).astype(jnp.bfloat16)
            part = lax.dot_general(
                scaled, a_ref[u, k, 1], (((1,), (1,)), ((), ())), preferred_element_type=jnp.float32
            )
            total = part if total is None else total + part
        for h in range(sides):
            held_ref[h, pl.ds(step * count + u, tile, stride=BATCH), :] = total[:, h * LANES:(h + 1) * LANES]

    @pl.when(step == pl.num_programs(1) - 1)
    def _():
        together = 4

        @pl.loop(0, n_down // together)
        def _(block):
            at = [(d, q, h) for d in range(together) for q in range(quads) for h in range(sides)]
            parts = []
            for d, q, h in at:
                row = ((block * together + d) * rows + q * per) * BATCH
                parts.append(jnp.concatenate([
                    held_ref[h, pl.ds(pl.multiple_of(row + r * BATCH, BATCH), BATCH), :].astype(jnp.bfloat16)
                    for r in range(per)
                ], axis=1))
            swapped = jnp.dot(
                jnp.concatenate(parts, axis=0), swap_ref[...], preferred_element_type=jnp.float32
            ).astype(jnp.bfloat16)
            for n, (d, q, h) in enumerate(at):
                for j in range(per):
                    first = block * (together * n_across) + device_of(d, h * per + j, n_across)
                    out_ref[first, :, q * LANES:(q + 1) * LANES] = (
                        swapped[n * BATCH:(n + 1) * BATCH, j * LANES:(j + 1) * LANES]
                    )


def form_products(a_tiles, scaling, swap, n_down, n_across):
    contribs, blocks, _, tile, _ = a_tiles.shape
    n_all = n_down * n_across
    chunk = tile * tile // n_all
    count = 8
    steps = BATCH // count
    return pl.pallas_call(
        functools.partial(products_kernel, n_down, n_across),
        grid=(contribs // BATCH, steps),
        in_specs=[
            pl.BlockSpec((count, blocks, 2, tile, tile), lambda g, s: (g * steps + s, 0, 0, 0, 0)),
            pl.BlockSpec((count, blocks, tile), lambda g, s: (g * steps + s, 0, 0)),
            pl.BlockSpec(swap.shape, lambda g, s: (0, 0)),
        ],
        out_specs=pl.BlockSpec((n_all, BATCH, chunk), lambda g, s: (0, g, 0)),
        out_shape=jax.ShapeDtypeStruct((n_all, contribs, chunk), jnp.bfloat16),
        scratch_shapes=[pltpu.VMEM((tile // LANES, tile * BATCH, LANES), jnp.float32)],
        compiler_params=VMEM,
    )(a_tiles, scaling, swap)


def sum_kernel(x_ref, target_ref, update_ref, out_ref, total_ref, spread_ref):
    step = pl.program_id(0)
    n_tiles, chunk = total_ref.shape
    number = lax.broadcasted_iota(jnp.int32, (n_tiles, x_ref.shape[0]), 0)
    picking = (number == target_ref[...]).astype(jnp.float32).astype(jnp.bfloat16)
    part = jnp.dot(picking, x_ref[...], preferred_element_type=jnp.float32)

    @pl.when(step == 0)
    def _():
        total_ref[...] = part - update_ref[...]

    @pl.when(step > 0)
    def _():
        total_ref[...] += part

    @pl.when(step == pl.num_programs(0) - 1)
    def _():
        pieces = chunk // LANES
        for q in range(pieces):
            spread_ref[pl.ds(q, n_tiles, stride=pieces), :] = total_ref[:, q * LANES:(q + 1) * LANES]
        out_ref[...] = spread_ref[...].astype(jnp.bfloat16)


def sum_by_target(x, target, update):
    contribs, chunk = x.shape
    n_tiles = update.shape[0]
    block = 1024
    return pl.pallas_call(
        sum_kernel,
        grid=(contribs // block,),
        in_specs=[
            pl.BlockSpec((block, chunk), lambda s: (s, 0)),
            pl.BlockSpec((1, block), lambda s: (0, s)),
            pl.BlockSpec((n_tiles, chunk), lambda s: (0, 0)),
        ],
        out_specs=pl.BlockSpec((n_tiles * chunk // LANES, LANES), lambda s: (0, 0)),
        out_shape=jax.ShapeDtypeStruct((n_tiles * chunk // LANES, LANES), jnp.bfloat16),
        scratch_shapes=[
            pltpu.VMEM((n_tiles, chunk), jnp.float32),
            pltpu.VMEM((n_tiles * chunk // LANES, LANES), jnp.float32),
        ],
        compiler_params=VMEM,
    )(x, target.reshape(1, -1), update)


def final_kernel(n_down, n_across, x_ref, swap_ref, out_ref, spread_ref):
    held, tile, _ = out_ref.shape
    rows, cols = tile // n_down, tile // n_across
    per = LANES // cols
    quads = rows // per
    sides = tile // LANES
    at = [(i, h) for i in range(n_down) for h in range(sides)]
    parts = []
    for i, h in at:
        parts.append(jnp.concatenate([x_ref[device_of(i, h * per + j, n_across)] for j in range(per)], axis=1))
    swapped = jnp.dot(jnp.concatenate(parts, axis=0), swap_ref[...], preferred_element_type=jnp.float32)
    for n, (i, h) in enumerate(at):
        for r in range(per):
            for s in range(held):
                top = n * held * quads + s * quads
                spread_ref[h, pl.ds(s * tile + i * rows + r, quads, stride=per), :] = (
                    swapped[top:top + quads, r * LANES:(r + 1) * LANES]
                )
    for s in range(held):
        for h in range(sides):
            out_ref[s, :, h * LANES:(h + 1) * LANES] = spread_ref[h, s * tile:(s + 1) * tile, :]


def final_tiles(x, swap, tile, held, n_down, n_across):
    vmem = pl.BlockSpec(memory_space=pltpu.VMEM)
    return pl.pallas_call(
        functools.partial(final_kernel, n_down, n_across),
        in_specs=[vmem, vmem],
        out_specs=vmem,
        out_shape=jax.ShapeDtypeStruct((held, tile, tile), jnp.float32),
        scratch_shapes=[pltpu.VMEM((tile // LANES, held * tile, LANES), jnp.float32)],
        compiler_params=VMEM,
    )(x, swap)


def per_device(a_tiles, scaling, dest_owner, dest_slot, panel, front_tiles):
    contribs, _, _, tile, _ = a_tiles.shape
    n_group, n_chip, n_core = (lax.axis_size(name) for name in AXES)
    n_dev = n_chip * n_core
    n_all = n_dev * n_group
    held = front_tiles.shape[0]
    n_tiles = n_all * held
    n_across = 8
    n_down = n_all // n_across
    rows, cols = tile // n_down, tile // n_across
    chunk = rows * cols
    depth = panel.shape[1]
    swap = swap_matrix(LANES // cols)

    early = exchange(early_blocks(dest_owner[:, 0], dest_slot, front_tiles, panel, n_down, n_across), PLANE)
    arrived = exchange(form_products(a_tiles, scaling, swap, n_down, n_across), AXES)

    even = lax.axis_index("core") == 0
    low, high, rest = early[:, :rows], early[:, rows:2 * rows], early[:, 2 * rows:]
    own = jnp.concatenate([jnp.where(even, low, high), rest], axis=1)
    other = jnp.concatenate([jnp.where(even, high, low), rest], axis=1)
    other = lax.ppermute(other, "core", [(0, 1), (1, 0)])
    early = jnp.where(even, jnp.stack([own, other], axis=1), jnp.stack([other, own], axis=1))
    early = early.reshape(n_group, n_dev, -1, depth)

    numbers = early[:, :, rows + cols].astype(jnp.int32).reshape(n_all, depth)
    owner, slot = numbers[:, :contribs].reshape(-1), numbers[:, contribs:2 * contribs].reshape(-1)
    target = (slot // held) * (n_dev * held) + owner * held + slot % held
    first = 2 * contribs
    row_piece = numbers[:, first:first + held].reshape(-1)
    col_piece = numbers[:, first + held:first + 2 * held].reshape(-1)

    grid = jnp.einsum(
        "glrp,gsmp->lsrm", early[:, :, :rows], early[:, :, rows:rows + cols], preferred_element_type=jnp.float32
    ).reshape(n_dev * n_dev, chunk)
    update = jnp.take(grid, row_piece * n_dev + col_piece, axis=0, mode="clip")

    sums = sum_by_target(arrived.reshape(n_all * contribs, chunk), target, update)
    final = exchange(sums.reshape(n_all, held * chunk // LANES, LANES), AXES)
    return final_tiles(final, swap, tile, held, n_down, n_across)


def solution(mesh):
    n_group, n_dev = mesh.devices.shape
    mesh = jax.sharding.Mesh(mesh.devices.reshape(n_group, n_dev // 2, 2), AXES)
    in_specs = (
        P(AXES, None, None, None, None),
        P(AXES, None, None),
        P(AXES, None),
        P(AXES),
        P(("chip", "core"), "group"),
        P(AXES, None),
    )
    out_specs = P(AXES, None, None)
    return jax.shard_map(
        per_device, mesh=mesh, in_specs=in_specs, out_specs=out_specs, check_vma=False
    )
```

```python
import functools
import jax
import jax.numpy as jnp
from jax import lax
from jax.experimental import pallas as pl
from jax.experimental.pallas import tpu as pltpu
from jax.sharding import PartitionSpec as P

AXES = ("group", "chip", "core")
PLANE = ("group", "chip")
LANES = 128
BATCH = 16
VMEM = pltpu.CompilerParams(vmem_limit_bytes=48 << 20)


def exchange(x, axes):
    return lax.all_to_all(x, axes, split_axis=0, concat_axis=0, tiled=True)


def device_of(i, j, n_across):
    return (i // 2) * (2 * n_across) + 2 * j + i % 2


def pick_lanes(parts, shift, per):
    group = lax.broadcasted_iota(jnp.int32, parts[0].shape, 1) // (LANES // per)
    result = parts[0]
    for n in range(1, per):
        result = jnp.where(group == (shift + n) % per, parts[n], result)
    return result


def early_kernel(n_down, n_across, owner_hbm, slot_hbm, front_hbm, panel_hbm, out_ref,
                 owner_ref, slot_ref, front_ref, panel_ref, sem_ref):
    pairs = [(owner_hbm, owner_ref), (slot_hbm, slot_ref), (front_hbm, front_ref), (panel_hbm, panel_ref)]
    copies = [pltpu.make_async_copy(a, b, sem_ref.at[n]) for n, (a, b) in enumerate(pairs)]
    for copy in copies:
        copy.start()
    for copy in copies:
        copy.wait()
    tile, depth = panel_ref.shape
    rows = tile // n_down
    count = owner_ref.shape[0]
    held = front_ref.shape[1]
    lane = lax.broadcasted_iota(jnp.int32, (8, depth), 1)
    numbers = jnp.zeros((8, depth), jnp.int32)
    for c in range(count):
        numbers = jnp.where(lane == c, owner_ref[c], numbers)
        numbers = jnp.where(lane == count + c, slot_ref[c], numbers)
    for s in range(held):
        for side in range(2):
            numbers = jnp.where(lane == 2 * count + side * held + s, front_ref[side, s], numbers)
    numbers = numbers.astype(jnp.float32).astype(jnp.bfloat16)
    cols = tile // n_across
    for a in range(n_down // 2):
        for j in range(n_across):
            chip = a * n_across + j
            out_ref[chip, 0:2 * rows, :] = panel_ref[2 * a * rows:2 * (a + 1) * rows, :]
            out_ref[chip, 2 * rows:2 * rows + cols, :] = panel_ref[j * cols:(j + 1) * cols, :]
            out_ref[chip, 2 * rows + cols:2 * rows + cols + 8, :] = numbers


def early_blocks(owner, slot, front_tiles, panel, n_down, n_across):
    tile, depth = panel.shape
    height = 2 * (tile // n_down) + tile // n_across + 8
    front = front_tiles.T
    hbm = pl.BlockSpec(memory_space=pltpu.HBM)
    return pl.pallas_call(
        functools.partial(early_kernel, n_down, n_across),
        in_specs=[hbm] * 4,
        out_specs=pl.BlockSpec(memory_space=pltpu.VMEM),
        out_shape=jax.ShapeDtypeStruct((n_down * n_across // 2, height, depth), jnp.bfloat16),
        scratch_shapes=[
            pltpu.SMEM(owner.shape, owner.dtype),
            pltpu.SMEM(slot.shape, slot.dtype),
            pltpu.SMEM(front.shape, front.dtype),
            pltpu.VMEM(panel.shape, panel.dtype),
            pltpu.SemaphoreType.DMA((4,)),
        ],
        compiler_params=pltpu.CompilerParams(vmem_limit_bytes=64 << 20),
    )(owner, slot, front, panel)


def products_kernel(n_down, n_across, a_ref, scale_ref, out_ref, held_ref):
    count, blocks, _, tile, _ = a_ref.shape
    rows, cols = tile // n_down, tile // n_across
    per = LANES // cols
    quads = rows // per
    sides = tile // LANES
    step = pl.program_id(1)
    for u in range(count):
        total = None
        for k in range(blocks):
            scaled = (a_ref[u, k, 0].astype(jnp.float32) * scale_ref[u, k][None, :]).astype(jnp.bfloat16)
            part = lax.dot_general(
                scaled, a_ref[u, k, 1], (((1,), (1,)), ((), ())), preferred_element_type=jnp.float32
            )
            total = part if total is None else total + part
        for h in range(sides):
            held_ref[h, pl.ds(step * count + u, tile, stride=BATCH), :] = total[:, h * LANES:(h + 1) * LANES]

    @pl.when(step == pl.num_programs(1) - 1)
    def _():
        @pl.loop(0, n_down // 2)
        def _(pair):
            for d in range(2):
                for q in range(quads):
                    for h in range(sides):
                        parts = []
                        for r in range(per):
                            row = ((pair * 2 + d) * rows + q * per + r) * BATCH
                            part = held_ref[h, pl.ds(pl.multiple_of(row, BATCH), BATCH), :]
                            parts.append(pltpu.roll(part, cols * r, axis=1) if r else part)
                        for j in range(per):
                            first = pair * (2 * n_across) + device_of(d, h * per + j, n_across)
                            out_ref[first, :, q * LANES:(q + 1) * LANES] = pick_lanes(parts, j, per).astype(jnp.bfloat16)


def form_products(a_tiles, scaling, n_down, n_across):
    contribs, blocks, _, tile, _ = a_tiles.shape
    n_all = n_down * n_across
    chunk = tile * tile // n_all
    count = 8
    steps = BATCH // count
    return pl.pallas_call(
        functools.partial(products_kernel, n_down, n_across),
        grid=(contribs // BATCH, steps),
        in_specs=[
            pl.BlockSpec((count, blocks, 2, tile, tile), lambda g, s: (g * steps + s, 0, 0, 0, 0)),
            pl.BlockSpec((count, blocks, tile), lambda g, s: (g * steps + s, 0, 0)),
        ],
        out_specs=pl.BlockSpec((n_all, BATCH, chunk), lambda g, s: (0, g, 0)),
        out_shape=jax.ShapeDtypeStruct((n_all, contribs, chunk), jnp.bfloat16),
        scratch_shapes=[pltpu.VMEM((tile // LANES, tile * BATCH, LANES), jnp.float32)],
        compiler_params=pltpu.CompilerParams(vmem_limit_bytes=64 << 20),
    )(a_tiles, scaling)


def sum_kernel(x_ref, target_ref, update_ref, out_ref, spread_ref):
    n_tiles, chunk = update_ref.shape
    number = lax.broadcasted_iota(jnp.int32, (n_tiles, x_ref.shape[0]), 0)
    picking = jnp.where(number == target_ref[...], 1.0, 0.0).astype(jnp.bfloat16)
    total = jnp.dot(picking, x_ref[...], preferred_element_type=jnp.float32) - update_ref[...]
    pieces = chunk // LANES
    for q in range(pieces):
        spread_ref[pl.ds(q, n_tiles, stride=pieces), :] = total[:, q * LANES:(q + 1) * LANES]
    out_ref[...] = spread_ref[...].astype(jnp.bfloat16)


def sum_by_target(x, target, update):
    contribs, chunk = x.shape
    n_tiles = update.shape[0]
    vmem = pl.BlockSpec(memory_space=pltpu.VMEM)
    return pl.pallas_call(
        sum_kernel,
        in_specs=[vmem, vmem, vmem],
        out_specs=vmem,
        out_shape=jax.ShapeDtypeStruct((n_tiles * chunk // LANES, LANES), jnp.bfloat16),
        scratch_shapes=[pltpu.VMEM((n_tiles * chunk // LANES, LANES), jnp.float32)],
        compiler_params=VMEM,
    )(x, target.reshape(1, -1), update)


def final_kernel(n_down, n_across, x_ref, out_ref, spread_ref):
    held, tile, _ = out_ref.shape
    rows, cols = tile // n_down, tile // n_across
    per = LANES // cols
    quads = rows // per
    sides = tile // LANES
    for i in range(n_down):
        for h in range(sides):
            parts = [x_ref[device_of(i, h * per + j, n_across)].astype(jnp.float32) for j in range(per)]
            for r in range(per):
                picked = pick_lanes(parts, r, per)
                if r:
                    picked = pltpu.roll(picked, LANES - cols * r, axis=1)
                for s in range(held):
                    spread_ref[h, pl.ds(s * tile + i * rows + r, quads, stride=per), :] = (
                        picked[s * quads:(s + 1) * quads]
                    )
    for s in range(held):
        for h in range(sides):
            out_ref[s, :, h * LANES:(h + 1) * LANES] = spread_ref[h, s * tile:(s + 1) * tile, :]


def final_tiles(x, tile, held, n_down, n_across):
    vmem = pl.BlockSpec(memory_space=pltpu.VMEM)
    return pl.pallas_call(
        functools.partial(final_kernel, n_down, n_across),
        in_specs=[vmem],
        out_specs=vmem,
        out_shape=jax.ShapeDtypeStruct((held, tile, tile), jnp.float32),
        scratch_shapes=[pltpu.VMEM((tile // LANES, held * tile, LANES), jnp.float32)],
        compiler_params=VMEM,
    )(x)


def per_device(a_tiles, scaling, dest_owner, dest_slot, panel, front_tiles):
    contribs, _, _, tile, _ = a_tiles.shape
    n_group, n_chip, n_core = (lax.axis_size(name) for name in AXES)
    n_dev = n_chip * n_core
    n_all = n_dev * n_group
    held = front_tiles.shape[0]
    n_tiles = n_all * held
    n_across = 8
    n_down = n_all // n_across
    rows, cols = tile // n_down, tile // n_across
    chunk = rows * cols
    depth = panel.shape[1]

    early = exchange(early_blocks(dest_owner[:, 0], dest_slot, front_tiles, panel, n_down, n_across), PLANE)
    arrived = exchange(form_products(a_tiles, scaling, n_down, n_across), AXES)

    even = lax.axis_index("core") == 0
    low, high, rest = early[:, :rows], early[:, rows:2 * rows], early[:, 2 * rows:]
    own = jnp.concatenate([jnp.where(even, low, high), rest], axis=1)
    other = jnp.concatenate([jnp.where(even, high, low), rest], axis=1)
    other = lax.ppermute(other, "core", [(0, 1), (1, 0)])
    early = jnp.where(even, jnp.stack([own, other], axis=1), jnp.stack([other, own], axis=1))
    early = early.reshape(n_group, n_dev, -1, depth)

    numbers = early[:, :, rows + cols].astype(jnp.int32).reshape(n_all, depth)
    owner, slot = numbers[:, :contribs].reshape(-1), numbers[:, contribs:2 * contribs].reshape(-1)
    target = (slot // held) * (n_dev * held) + owner * held + slot % held
    first = 2 * contribs
    row_piece = numbers[:, first:first + held].reshape(-1)
    col_piece = numbers[:, first + held:first + 2 * held].reshape(-1)

    per = LANES // cols
    chip = lax.axis_index("group") * n_chip + lax.axis_index("chip")
    left = early[:, :, :rows].reshape(n_group, n_dev, rows // per, per, depth)
    left = jnp.roll(left, chip % per, axis=3).reshape(n_group, n_dev, rows, depth)
    grid = jnp.einsum(
        "glrp,gsmp->lsrm", left, early[:, :, rows:rows + cols], preferred_element_type=jnp.float32
    ).reshape(n_dev * n_dev, chunk)
    update = jnp.take(grid, row_piece * n_dev + col_piece, axis=0, mode="clip")

    sums = sum_by_target(arrived.reshape(n_all * contribs, chunk), target, update)
    final = exchange(sums.reshape(n_all, held * chunk // LANES, LANES), AXES)
    return final_tiles(final, tile, held, n_down, n_across)


def solution(mesh):
    n_group, n_dev = mesh.devices.shape
    mesh = jax.sharding.Mesh(mesh.devices.reshape(n_group, n_dev // 2, 2), AXES)
    in_specs = (
        P(AXES, None, None, None, None),
        P(AXES, None, None),
        P(AXES, None),
        P(AXES),
        P(("chip", "core"), "group"),
        P(AXES, None),
    )
    out_specs = P(AXES, None, None)
    return jax.shard_map(
        per_device, mesh=mesh, in_specs=in_specs, out_specs=out_specs, check_vma=False
    )
```

```python
import functools
import jax
import jax.numpy as jnp
from jax import lax
from jax.experimental import pallas as pl
from jax.experimental.pallas import tpu as pltpu
from jax.sharding import PartitionSpec as P

AXES = ("group", "chip", "core")
PLANE = ("group", "chip")
LANES = 128
BATCH = 16
VMEM = pltpu.CompilerParams(vmem_limit_bytes=48 << 20)


def exchange(x, axes):
    return lax.all_to_all(x, axes, split_axis=0, concat_axis=0, tiled=True)


def device_of(i, j, n_across):
    return (i // 2) * (2 * n_across) + 2 * j + i % 2


def pick_lanes(parts, shift, per):
    group = lax.broadcasted_iota(jnp.int32, parts[0].shape, 1) // (LANES // per)
    result = parts[0]
    for n in range(1, per):
        result = jnp.where(group == (shift + n) % per, parts[n], result)
    return result


def early_kernel(n_down, n_across, owner_hbm, slot_hbm, front_hbm, panel_hbm, out_ref,
                 owner_ref, slot_ref, front_ref, panel_ref, sem_ref):
    pairs = [(owner_hbm, owner_ref), (slot_hbm, slot_ref), (front_hbm, front_ref), (panel_hbm, panel_ref)]
    copies = [pltpu.make_async_copy(a, b, sem_ref.at[n]) for n, (a, b) in enumerate(pairs)]
    for copy in copies:
        copy.start()
    for copy in copies:
        copy.wait()
    tile, depth = panel_ref.shape
    rows = tile // n_down
    count = owner_ref.shape[0]
    held = front_ref.shape[1]
    lane = lax.broadcasted_iota(jnp.int32, (8, depth), 1)
    numbers = jnp.zeros((8, depth), jnp.int32)
    for c in range(count):
        numbers = jnp.where(lane == c, owner_ref[c], numbers)
        numbers = jnp.where(lane == count + c, slot_ref[c], numbers)
    for s in range(held):
        for side in range(2):
            numbers = jnp.where(lane == 2 * count + side * held + s, front_ref[side, s], numbers)
    numbers = numbers.astype(jnp.float32).astype(jnp.bfloat16)
    cols = tile // n_across
    for a in range(n_down // 2):
        for j in range(n_across):
            chip = a * n_across + j
            out_ref[chip, 0:2 * rows, :] = panel_ref[2 * a * rows:2 * (a + 1) * rows, :]
            out_ref[chip, 2 * rows:2 * rows + cols, :] = panel_ref[j * cols:(j + 1) * cols, :]
            out_ref[chip, 2 * rows + cols:2 * rows + cols + 8, :] = numbers


def early_blocks(owner, slot, front_tiles, panel, n_down, n_across):
    tile, depth = panel.shape
    height = 2 * (tile // n_down) + tile // n_across + 8
    front = front_tiles.T
    hbm = pl.BlockSpec(memory_space=pltpu.HBM)
    return pl.pallas_call(
        functools.partial(early_kernel, n_down, n_across),
        in_specs=[hbm] * 4,
        out_specs=pl.BlockSpec(memory_space=pltpu.VMEM),
        out_shape=jax.ShapeDtypeStruct((n_down * n_across // 2, height, depth), jnp.bfloat16),
        scratch_shapes=[
            pltpu.SMEM(owner.shape, owner.dtype),
            pltpu.SMEM(slot.shape, slot.dtype),
            pltpu.SMEM(front.shape, front.dtype),
            pltpu.VMEM(panel.shape, panel.dtype),
            pltpu.SemaphoreType.DMA((4,)),
        ],
        compiler_params=pltpu.CompilerParams(vmem_limit_bytes=64 << 20),
    )(owner, slot, front, panel)


def products_kernel(n_down, n_across, a_ref, scale_ref, out_ref, held_ref):
    count, blocks, _, tile, _ = a_ref.shape
    rows, cols = tile // n_down, tile // n_across
    per = LANES // cols
    quads = rows // per
    sides = tile // LANES
    step = pl.program_id(1)
    for u in range(count):
        total = None
        for k in range(blocks):
            scaled = (a_ref[u, k, 0].astype(jnp.float32) * scale_ref[u, k][None, :]).astype(jnp.bfloat16)
            part = lax.dot_general(
                scaled, a_ref[u, k, 1], (((1,), (1,)), ((), ())), preferred_element_type=jnp.float32
            )
            total = part if total is None else total + part
        for h in range(sides):
            held_ref[h, pl.ds(step * count + u, tile, stride=BATCH), :] = total[:, h * LANES:(h + 1) * LANES]

    @pl.when(step == pl.num_programs(1) - 1)
    def _():
        @pl.loop(0, n_down // 2)
        def _(pair):
            for d in range(2):
                for q in range(quads):
                    for h in range(sides):
                        parts = []
                        for r in range(per):
                            row = ((pair * 2 + d) * rows + q * per + r) * BATCH
                            part = held_ref[h, pl.ds(pl.multiple_of(row, BATCH), BATCH), :]
                            parts.append(pltpu.roll(part, cols * r, axis=1) if r else part)
                        for j in range(per):
                            first = pair * (2 * n_across) + device_of(d, h * per + j, n_across)
                            out_ref[first, :, q * LANES:(q + 1) * LANES] = pick_lanes(parts, j, per).astype(jnp.bfloat16)


def form_products(a_tiles, scaling, n_down, n_across):
    contribs, blocks, _, tile, _ = a_tiles.shape
    n_all = n_down * n_across
    chunk = tile * tile // n_all
    count = 8
    steps = BATCH // count
    return pl.pallas_call(
        functools.partial(products_kernel, n_down, n_across),
        grid=(contribs // BATCH, steps),
        in_specs=[
            pl.BlockSpec((count, blocks, 2, tile, tile), lambda g, s: (g * steps + s, 0, 0, 0, 0)),
            pl.BlockSpec((count, blocks, tile), lambda g, s: (g * steps + s, 0, 0)),
        ],
        out_specs=pl.BlockSpec((n_all, BATCH, chunk), lambda g, s: (0, g, 0)),
        out_shape=jax.ShapeDtypeStruct((n_all, contribs, chunk), jnp.bfloat16),
        scratch_shapes=[pltpu.VMEM((tile // LANES, tile * BATCH, LANES), jnp.float32)],
        compiler_params=pltpu.CompilerParams(vmem_limit_bytes=64 << 20),
    )(a_tiles, scaling)


def sum_kernel(x_hbm, target_ref, update_ref, out_ref, x_ref, spread_ref, sem_ref):
    n_tiles, chunk = update_ref.shape
    parts = sem_ref.shape[0]
    share = x_ref.shape[0] // parts
    copies = []
    for n in range(parts):
        at = pl.ds(n * share, share)
        copies.append(pltpu.make_async_copy(x_hbm.at[at], x_ref.at[at], sem_ref.at[n]))
        copies[n].start()
    number = lax.broadcasted_iota(jnp.int32, (n_tiles, share), 0)
    total = -update_ref[...]
    for n in range(parts):
        at = slice(n * share, (n + 1) * share)
        picking = jnp.where(number == target_ref[:, at], 1.0, 0.0).astype(jnp.bfloat16)
        copies[n].wait()
        total += jnp.dot(picking, x_ref[at, :], preferred_element_type=jnp.float32)
    pieces = chunk // LANES
    for q in range(pieces):
        spread_ref[pl.ds(q, n_tiles, stride=pieces), :] = total[:, q * LANES:(q + 1) * LANES]
    out_ref[...] = spread_ref[...].astype(jnp.bfloat16)


def sum_by_target(x, target, update):
    n_tiles, chunk = update.shape
    vmem = pl.BlockSpec(memory_space=pltpu.VMEM)
    return pl.pallas_call(
        sum_kernel,
        in_specs=[pl.BlockSpec(memory_space=pltpu.HBM), vmem, vmem],
        out_specs=vmem,
        out_shape=jax.ShapeDtypeStruct((n_tiles * chunk // LANES, LANES), jnp.bfloat16),
        scratch_shapes=[
            pltpu.VMEM(x.shape, x.dtype),
            pltpu.VMEM((n_tiles * chunk // LANES, LANES), jnp.float32),
            pltpu.SemaphoreType.DMA((4,)),
        ],
        compiler_params=VMEM,
    )(x, target.reshape(1, -1), update)


def final_kernel(n_down, n_across, x_ref, out_ref, spread_ref):
    held, tile, _ = out_ref.shape
    rows, cols = tile // n_down, tile // n_across
    per = LANES // cols
    quads = rows // per
    sides = tile // LANES
    for i in range(n_down):
        for h in range(sides):
            parts = [x_ref[device_of(i, h * per + j, n_across)].astype(jnp.float32) for j in range(per)]
            for r in range(per):
                picked = pick_lanes(parts, r, per)
                if r:
                    picked = pltpu.roll(picked, LANES - cols * r, axis=1)
                for s in range(held):
                    spread_ref[h, pl.ds(s * tile + i * rows + r, quads, stride=per), :] = (
                        picked[s * quads:(s + 1) * quads]
                    )
    for s in range(held):
        for h in range(sides):
            out_ref[s, :, h * LANES:(h + 1) * LANES] = spread_ref[h, s * tile:(s + 1) * tile, :]


def final_tiles(x, tile, held, n_down, n_across):
    vmem = pl.BlockSpec(memory_space=pltpu.VMEM)
    return pl.pallas_call(
        functools.partial(final_kernel, n_down, n_across),
        in_specs=[vmem],
        out_specs=vmem,
        out_shape=jax.ShapeDtypeStruct((held, tile, tile), jnp.float32),
        scratch_shapes=[pltpu.VMEM((tile // LANES, held * tile, LANES), jnp.float32)],
        compiler_params=VMEM,
    )(x)


def per_device(a_tiles, scaling, dest_owner, dest_slot, panel, front_tiles):
    contribs, _, _, tile, _ = a_tiles.shape
    n_group, n_chip, n_core = (lax.axis_size(name) for name in AXES)
    n_dev = n_chip * n_core
    n_all = n_dev * n_group
    held = front_tiles.shape[0]
    n_tiles = n_all * held
    n_across = 8
    n_down = n_all // n_across
    rows, cols = tile // n_down, tile // n_across
    chunk = rows * cols
    depth = panel.shape[1]

    early = exchange(early_blocks(dest_owner[:, 0], dest_slot, front_tiles, panel, n_down, n_across), PLANE)
    arrived = exchange(form_products(a_tiles, scaling, n_down, n_across), AXES)

    even = lax.axis_index("core") == 0
    low, high, rest = early[:, :rows], early[:, rows:2 * rows], early[:, 2 * rows:]
    own = jnp.concatenate([jnp.where(even, low, high), rest], axis=1)
    other = jnp.concatenate([jnp.where(even, high, low), rest], axis=1)
    other = lax.ppermute(other, "core", [(0, 1), (1, 0)])
    early = jnp.where(even, jnp.stack([own, other], axis=1), jnp.stack([other, own], axis=1))
    early = early.reshape(n_group, n_dev, -1, depth)

    numbers = early[:, :, rows + cols].astype(jnp.int32).reshape(n_all, depth)
    owner, slot = numbers[:, :contribs].reshape(-1), numbers[:, contribs:2 * contribs].reshape(-1)
    target = (slot // held) * (n_dev * held) + owner * held + slot % held
    first = 2 * contribs
    row_piece = numbers[:, first:first + held].reshape(-1)
    col_piece = numbers[:, first + held:first + 2 * held].reshape(-1)

    per = LANES // cols
    chip = lax.axis_index("group") * n_chip + lax.axis_index("chip")
    left = early[:, :, :rows].reshape(n_group, n_dev, rows // per, per, depth)
    left = jnp.roll(left, chip % per, axis=3).reshape(n_group, n_dev, rows, depth)
    grid = jnp.einsum(
        "glrp,gsmp->lsrm", left, early[:, :, rows:rows + cols], preferred_element_type=jnp.float32
    ).reshape(n_dev * n_dev, chunk)
    update = jnp.take(grid, row_piece * n_dev + col_piece, axis=0, mode="clip")

    sums = sum_by_target(arrived.reshape(n_all * contribs, chunk), target, update)
    final = exchange(sums.reshape(n_all, held * chunk // LANES, LANES), AXES)
    return final_tiles(final, tile, held, n_down, n_across)


def solution(mesh):
    n_group, n_dev = mesh.devices.shape
    mesh = jax.sharding.Mesh(mesh.devices.reshape(n_group, n_dev // 2, 2), AXES)
    in_specs = (
        P(AXES, None, None, None, None),
        P(AXES, None, None),
        P(AXES, None),
        P(AXES),
        P(("chip", "core"), "group"),
        P(AXES, None),
    )
    out_specs = P(AXES, None, None)
    return jax.shard_map(
        per_device, mesh=mesh, in_specs=in_specs, out_specs=out_specs, check_vma=False
    )
```

```python
import functools
import jax
import jax.numpy as jnp
from jax import lax
from jax.experimental import pallas as pl
from jax.experimental.pallas import tpu as pltpu
from jax.sharding import PartitionSpec as P

AXES = ("group", "chip", "core")
PLANE = ("group", "chip")
LANES = 128
BATCH = 16
VMEM = pltpu.CompilerParams(vmem_limit_bytes=48 << 20)


def exchange(x, axes):
    return lax.all_to_all(x, axes, split_axis=0, concat_axis=0, tiled=True)


def device_of(i, j, n_across):
    return (i // 2) * (2 * n_across) + 2 * j + i % 2


def pick_lanes(parts, shift, per):
    group = lax.broadcasted_iota(jnp.int32, parts[0].shape, 1) // (LANES // per)
    result = parts[0]
    for n in range(1, per):
        result = jnp.where(group == (shift + n) % per, parts[n], result)
    return result


def early_kernel(n_down, n_across, owner_hbm, slot_hbm, front_hbm, panel_hbm, out_ref,
                 owner_ref, slot_ref, front_ref, panel_ref, sem_ref):
    pairs = [(owner_hbm, owner_ref), (slot_hbm, slot_ref), (front_hbm, front_ref), (panel_hbm, panel_ref)]
    copies = [pltpu.make_async_copy(a, b, sem_ref.at[n]) for n, (a, b) in enumerate(pairs)]
    for copy in copies:
        copy.start()
    for copy in copies:
        copy.wait()
    tile, depth = panel_ref.shape
    rows = tile // n_down
    count = owner_ref.shape[0]
    held = front_ref.shape[1]
    lane = lax.broadcasted_iota(jnp.int32, (8, depth), 1)
    numbers = jnp.zeros((8, depth), jnp.int32)
    for c in range(count):
        numbers = jnp.where(lane == c, owner_ref[c], numbers)
        numbers = jnp.where(lane == count + c, slot_ref[c], numbers)
    for s in range(held):
        for side in range(2):
            numbers = jnp.where(lane == 2 * count + side * held + s, front_ref[side, s], numbers)
    numbers = numbers.astype(jnp.float32).astype(jnp.bfloat16)
    cols = tile // n_across
    for a in range(n_down // 2):
        for j in range(n_across):
            chip = a * n_across + j
            out_ref[chip, 0:2 * rows, :] = panel_ref[2 * a * rows:2 * (a + 1) * rows, :]
            out_ref[chip, 2 * rows:2 * rows + cols, :] = panel_ref[j * cols:(j + 1) * cols, :]
            out_ref[chip, 2 * rows + cols:2 * rows + cols + 8, :] = numbers


def early_blocks(owner, slot, front_tiles, panel, n_down, n_across):
    tile, depth = panel.shape
    height = 2 * (tile // n_down) + tile // n_across + 8
    front = front_tiles.T
    hbm = pl.BlockSpec(memory_space=pltpu.HBM)
    return pl.pallas_call(
        functools.partial(early_kernel, n_down, n_across),
        in_specs=[hbm] * 4,
        out_specs=pl.BlockSpec(memory_space=pltpu.VMEM),
        out_shape=jax.ShapeDtypeStruct((n_down * n_across // 2, height, depth), jnp.bfloat16),
        scratch_shapes=[
            pltpu.SMEM(owner.shape, owner.dtype),
            pltpu.SMEM(slot.shape, slot.dtype),
            pltpu.SMEM(front.shape, front.dtype),
            pltpu.VMEM(panel.shape, panel.dtype),
            pltpu.SemaphoreType.DMA((4,)),
        ],
        compiler_params=pltpu.CompilerParams(vmem_limit_bytes=64 << 20),
    )(owner, slot, front, panel)


def products_kernel(n_down, n_across, a_ref, scale_ref, out_ref, held_ref):
    count, blocks, _, tile, _ = a_ref.shape
    rows, cols = tile // n_down, tile // n_across
    per = LANES // cols
    quads = rows // per
    sides = tile // LANES
    step = pl.program_id(1)
    for u in range(count):
        total = None
        for k in range(blocks):
            scaled = (a_ref[u, k, 0].astype(jnp.float32) * scale_ref[u, k][None, :]).astype(jnp.bfloat16)
            part = lax.dot_general(
                scaled, a_ref[u, k, 1], (((1,), (1,)), ((), ())), preferred_element_type=jnp.float32
            )
            total = part if total is None else total + part
        for h in range(sides):
            held_ref[h, pl.ds(step * count + u, tile, stride=BATCH), :] = total[:, h * LANES:(h + 1) * LANES]

    @pl.when(step == pl.num_programs(1) - 1)
    def _():
        @pl.loop(0, n_down // 2)
        def _(pair):
            for d in range(2):
                for q in range(quads):
                    for h in range(sides):
                        parts = []
                        for r in range(per):
                            row = ((pair * 2 + d) * rows + q * per + r) * BATCH
                            part = held_ref[h, pl.ds(pl.multiple_of(row, BATCH), BATCH), :]
                            parts.append(pltpu.roll(part, cols * r, axis=1) if r else part)
                        for j in range(per):
                            first = pair * (2 * n_across) + device_of(d, h * per + j, n_across)
                            out_ref[first, :, q * LANES:(q + 1) * LANES] = pick_lanes(parts, j, per).astype(jnp.bfloat16)


def form_products(a_tiles, scaling, n_down, n_across):
    contribs, blocks, _, tile, _ = a_tiles.shape
    n_all = n_down * n_across
    chunk = tile * tile // n_all
    count = 8
    steps = BATCH // count
    return pl.pallas_call(
        functools.partial(products_kernel, n_down, n_across),
        grid=(contribs // BATCH, steps),
        in_specs=[
            pl.BlockSpec((count, blocks, 2, tile, tile), lambda g, s: (g * steps + s, 0, 0, 0, 0)),
            pl.BlockSpec((count, blocks, tile), lambda g, s: (g * steps + s, 0, 0)),
        ],
        out_specs=pl.BlockSpec((n_all, BATCH, chunk), lambda g, s: (0, g, 0)),
        out_shape=jax.ShapeDtypeStruct((n_all, contribs, chunk), jnp.bfloat16),
        scratch_shapes=[pltpu.VMEM((tile // LANES, (tile + 1) * BATCH, LANES), jnp.float32)],
        compiler_params=pltpu.CompilerParams(vmem_limit_bytes=64 << 20),
    )(a_tiles, scaling)


def sum_kernel(x_hbm, target_ref, update_ref, out_ref, x_ref, spread_ref, sem_ref):
    n_tiles, chunk = update_ref.shape
    parts = sem_ref.shape[0]
    share = x_ref.shape[0] // parts
    copies = []
    for n in range(parts):
        at = pl.ds(n * share, share)
        copies.append(pltpu.make_async_copy(x_hbm.at[at], x_ref.at[at], sem_ref.at[n]))
        copies[n].start()
    number = lax.broadcasted_iota(jnp.int32, (n_tiles, share), 0)
    total = -update_ref[...]
    for n in range(parts):
        at = slice(n * share, (n + 1) * share)
        picking = jnp.where(number == target_ref[:, at], 1.0, 0.0).astype(jnp.bfloat16)
        copies[n].wait()
        total += jnp.dot(picking, x_ref[at, :], preferred_element_type=jnp.float32)
    pieces = chunk // LANES
    for q in range(pieces):
        spread_ref[pl.ds(q, n_tiles, stride=pieces), :] = total[:, q * LANES:(q + 1) * LANES]
    out_ref[...] = spread_ref[0:n_tiles * pieces, :].astype(jnp.bfloat16)


def sum_by_target(x, target, update):
    n_tiles, chunk = update.shape
    vmem = pl.BlockSpec(memory_space=pltpu.VMEM)
    return pl.pallas_call(
        sum_kernel,
        in_specs=[pl.BlockSpec(memory_space=pltpu.HBM), vmem, vmem],
        out_specs=vmem,
        out_shape=jax.ShapeDtypeStruct((n_tiles * chunk // LANES, LANES), jnp.bfloat16),
        scratch_shapes=[
            pltpu.VMEM(x.shape, x.dtype),
            pltpu.VMEM((n_tiles * chunk // LANES + 8, LANES), jnp.float32),
            pltpu.SemaphoreType.DMA((4,)),
        ],
        compiler_params=VMEM,
    )(x, target.reshape(1, -1), update)


def final_kernel(n_down, n_across, x_ref, out_ref, spread_ref):
    held, tile, _ = out_ref.shape
    rows, cols = tile // n_down, tile // n_across
    per = LANES // cols
    quads = rows // per
    sides = tile // LANES
    for i in range(n_down):
        for h in range(sides):
            parts = [x_ref[device_of(i, h * per + j, n_across)].astype(jnp.float32) for j in range(per)]
            for r in range(per):
                picked = pick_lanes(parts, r, per)
                if r:
                    picked = pltpu.roll(picked, LANES - cols * r, axis=1)
                for s in range(held):
                    spread_ref[h, pl.ds(s * tile + i * rows + r, quads, stride=per), :] = (
                        picked[s * quads:(s + 1) * quads]
                    )
    for s in range(held):
        for h in range(sides):
            out_ref[s, :, h * LANES:(h + 1) * LANES] = spread_ref[h, s * tile:(s + 1) * tile, :]


def final_tiles(x, tile, held, n_down, n_across):
    vmem = pl.BlockSpec(memory_space=pltpu.VMEM)
    return pl.pallas_call(
        functools.partial(final_kernel, n_down, n_across),
        in_specs=[vmem],
        out_specs=vmem,
        out_shape=jax.ShapeDtypeStruct((held, tile, tile), jnp.float32),
        scratch_shapes=[pltpu.VMEM((tile // LANES, held * tile + 8, LANES), jnp.float32)],
        compiler_params=VMEM,
    )(x)


def per_device(a_tiles, scaling, dest_owner, dest_slot, panel, front_tiles):
    contribs, _, _, tile, _ = a_tiles.shape
    n_group, n_chip, n_core = (lax.axis_size(name) for name in AXES)
    n_dev = n_chip * n_core
    n_all = n_dev * n_group
    held = front_tiles.shape[0]
    n_tiles = n_all * held
    n_across = 8
    n_down = n_all // n_across
    rows, cols = tile // n_down, tile // n_across
    chunk = rows * cols
    depth = panel.shape[1]

    early = exchange(early_blocks(dest_owner[:, 0], dest_slot, front_tiles, panel, n_down, n_across), PLANE)
    arrived = exchange(form_products(a_tiles, scaling, n_down, n_across), AXES)

    even = lax.axis_index("core") == 0
    low, high, rest = early[:, :rows], early[:, rows:2 * rows], early[:, 2 * rows:]
    own = jnp.concatenate([jnp.where(even, low, high), rest], axis=1)
    other = jnp.concatenate([jnp.where(even, high, low), rest], axis=1)
    other = lax.ppermute(other, "core", [(0, 1), (1, 0)])
    early = jnp.where(even, jnp.stack([own, other], axis=1), jnp.stack([other, own], axis=1))
    early = early.reshape(n_group, n_dev, -1, depth)

    numbers = early[:, :, rows + cols].astype(jnp.int32).reshape(n_all, depth)
    owner, slot = numbers[:, :contribs].reshape(-1), numbers[:, contribs:2 * contribs].reshape(-1)
    target = (slot // held) * (n_dev * held) + owner * held + slot % held
    first = 2 * contribs
    row_piece = numbers[:, first:first + held].reshape(-1)
    col_piece = numbers[:, first + held:first + 2 * held].reshape(-1)

    per = LANES // cols
    chip = lax.axis_index("group") * n_chip + lax.axis_index("chip")
    left = early[:, :, :rows].reshape(n_group, n_dev, rows // per, per, depth)
    left = jnp.roll(left, chip % per, axis=3).reshape(n_group, n_dev, rows, depth)
    grid = jnp.einsum(
        "glrp,gsmp->lsrm", left, early[:, :, rows:rows + cols], preferred_element_type=jnp.float32
    ).reshape(n_dev * n_dev, chunk)
    update = jnp.take(grid, row_piece * n_dev + col_piece, axis=0, mode="clip")

    sums = sum_by_target(arrived.reshape(n_all * contribs, chunk), target, update)
    final = exchange(sums.reshape(n_all, held * chunk // LANES, LANES), AXES)
    return final_tiles(final, tile, held, n_down, n_across)


def solution(mesh):
    n_group, n_dev = mesh.devices.shape
    mesh = jax.sharding.Mesh(mesh.devices.reshape(n_group, n_dev // 2, 2), AXES)
    in_specs = (
        P(AXES, None, None, None, None),
        P(AXES, None, None),
        P(AXES, None),
        P(AXES),
        P(("chip", "core"), "group"),
        P(AXES, None),
    )
    out_specs = P(AXES, None, None)
    return jax.shard_map(
        per_device, mesh=mesh, in_specs=in_specs, out_specs=out_specs, check_vma=False
    )
```

```python
import functools
import jax
import jax.numpy as jnp
from jax import lax
from jax.experimental import pallas as pl
from jax.experimental.pallas import tpu as pltpu
from jax.sharding import PartitionSpec as P

AXES = ("group", "chip", "core")
PLANE = ("group", "chip")
LANES = 128
BATCH = 16
VMEM = pltpu.CompilerParams(vmem_limit_bytes=48 << 20)


def exchange(x, axes):
    return lax.all_to_all(x, axes, split_axis=0, concat_axis=0, tiled=True)


def device_of(i, j, n_across):
    return (i // 2) * (2 * n_across) + 2 * j + i % 2


def pick_lanes(parts, shift, per):
    group = lax.broadcasted_iota(jnp.int32, parts[0].shape, 1) // (LANES // per)
    result = parts[0]
    for n in range(1, per):
        result = jnp.where(group == (shift + n) % per, parts[n], result)
    return result


def early_kernel(n_down, n_across, owner_hbm, slot_hbm, front_hbm, panel_hbm, out_ref,
                 owner_ref, slot_ref, front_ref, panel_ref, sem_ref):
    pairs = [(owner_hbm, owner_ref), (slot_hbm, slot_ref), (front_hbm, front_ref), (panel_hbm, panel_ref)]
    copies = [pltpu.make_async_copy(a, b, sem_ref.at[n]) for n, (a, b) in enumerate(pairs)]
    for copy in copies:
        copy.start()
    for copy in copies:
        copy.wait()
    tile, depth = panel_ref.shape
    rows = tile // n_down
    count = owner_ref.shape[0]
    held = front_ref.shape[1]
    lane = lax.broadcasted_iota(jnp.int32, (8, depth), 1)
    numbers = jnp.zeros((8, depth), jnp.int32)
    for c in range(count):
        numbers = jnp.where(lane == c, owner_ref[c], numbers)
        numbers = jnp.where(lane == count + c, slot_ref[c], numbers)
    for s in range(held):
        for side in range(2):
            numbers = jnp.where(lane == 2 * count + side * held + s, front_ref[side, s], numbers)
    numbers = numbers.astype(jnp.float32).astype(jnp.bfloat16)
    cols = tile // n_across
    for a in range(n_down // 2):
        for j in range(n_across):
            chip = a * n_across + j
            out_ref[chip, 0:2 * rows, :] = panel_ref[2 * a * rows:2 * (a + 1) * rows, :]
            out_ref[chip, 2 * rows:2 * rows + cols, :] = panel_ref[j * cols:(j + 1) * cols, :]
            out_ref[chip, 2 * rows + cols:2 * rows + cols + 8, :] = numbers


def early_blocks(owner, slot, front_tiles, panel, n_down, n_across):
    tile, depth = panel.shape
    height = 2 * (tile // n_down) + tile // n_across + 8
    front = front_tiles.T
    hbm = pl.BlockSpec(memory_space=pltpu.HBM)
    return pl.pallas_call(
        functools.partial(early_kernel, n_down, n_across),
        in_specs=[hbm] * 4,
        out_specs=pl.BlockSpec(memory_space=pltpu.VMEM),
        out_shape=jax.ShapeDtypeStruct((n_down * n_across // 2, height, depth), jnp.bfloat16),
        scratch_shapes=[
            pltpu.SMEM(owner.shape, owner.dtype),
            pltpu.SMEM(slot.shape, slot.dtype),
            pltpu.SMEM(front.shape, front.dtype),
            pltpu.VMEM(panel.shape, panel.dtype),
            pltpu.SemaphoreType.DMA((4,)),
        ],
        compiler_params=pltpu.CompilerParams(vmem_limit_bytes=64 << 20),
    )(owner, slot, front, panel)


def products_kernel(n_down, n_across, a_ref, scale_ref, out_ref, held_ref):
    count, blocks, _, tile, _ = a_ref.shape
    rows, cols = tile // n_down, tile // n_across
    per = LANES // cols
    quads = rows // per
    sides = tile // LANES
    step = pl.program_id(1)
    for u in range(count):
        total = None
        for k in range(blocks):
            scaled = (a_ref[u, k, 0].astype(jnp.float32) * scale_ref[u, k][None, :]).astype(jnp.bfloat16)
            part = lax.dot_general(
                scaled, a_ref[u, k, 1], (((1,), (1,)), ((), ())), preferred_element_type=jnp.float32
            )
            total = part if total is None else total + part
        for h in range(sides):
            held_ref[h, pl.ds(step * count + u, tile, stride=BATCH), :] = total[:, h * LANES:(h + 1) * LANES]

    @pl.when(step == pl.num_programs(1) - 1)
    def _():
        @pl.loop(0, n_down // 2)
        def _(pair):
            for d in range(2):
                for q in range(quads):
                    for h in range(sides):
                        parts = []
                        for r in range(per):
                            row = ((pair * 2 + d) * rows + q * per + r) * BATCH
                            part = held_ref[h, pl.ds(pl.multiple_of(row, BATCH), BATCH), :]
                            parts.append(pltpu.roll(part, cols * r, axis=1) if r else part)
                        for j in range(per):
                            first = pair * (2 * n_across) + device_of(d, h * per + j, n_across)
                            out_ref[first, :, q * LANES:(q + 1) * LANES] = pick_lanes(parts, j, per).astype(jnp.bfloat16)


def form_products(a_tiles, scaling, n_down, n_across):
    contribs, blocks, _, tile, _ = a_tiles.shape
    n_all = n_down * n_across
    chunk = tile * tile // n_all
    count = 8
    steps = BATCH // count
    return pl.pallas_call(
        functools.partial(products_kernel, n_down, n_across),
        grid=(contribs // BATCH, steps),
        in_specs=[
            pl.BlockSpec((count, blocks, 2, tile, tile), lambda g, s: (g * steps + s, 0, 0, 0, 0)),
            pl.BlockSpec((count, blocks, tile), lambda g, s: (g * steps + s, 0, 0)),
        ],
        out_specs=pl.BlockSpec((n_all, BATCH, chunk), lambda g, s: (0, g, 0)),
        out_shape=jax.ShapeDtypeStruct((n_all, contribs, chunk), jnp.bfloat16),
        scratch_shapes=[pltpu.VMEM((tile // LANES, (tile + 1) * BATCH, LANES), jnp.float32)],
        compiler_params=pltpu.CompilerParams(vmem_limit_bytes=64 << 20),
    )(a_tiles, scaling)


def sum_kernel(x_hbm, target_ref, update_ref, *refs):
    ready_refs, (out_ref, x_ref, spread_ref, sem_ref) = refs[:-4], refs[-4:]
    n_tiles, chunk = update_ref.shape
    parts = sem_ref.shape[0]
    share = x_ref.shape[0] // parts
    own = parts - len(ready_refs)
    copies = []
    for n in range(parts):
        at = pl.ds(n * share, share)
        copies.append(pltpu.make_async_copy(x_hbm.at[at], x_ref.at[at], sem_ref.at[n]))
        copies[n].start()
    number = lax.broadcasted_iota(jnp.int32, (n_tiles, share), 0)
    total = -update_ref[...]
    for n in range(parts):
        at = slice(n * share, (n + 1) * share)
        if n < own:
            picking = jnp.where(number == target_ref[:, at], 1.0, 0.0).astype(jnp.bfloat16)
        else:
            picking = ready_refs[n - own][...]
        copies[n].wait()
        total += jnp.dot(picking, x_ref[at, :], preferred_element_type=jnp.float32)
    pieces = chunk // LANES
    for q in range(pieces):
        spread_ref[pl.ds(q, n_tiles, stride=pieces), :] = total[:, q * LANES:(q + 1) * LANES]
    out_ref[...] = spread_ref[0:n_tiles * pieces, :].astype(jnp.bfloat16)


def sum_by_target(x, target, update):
    n_tiles, chunk = update.shape
    parts, own = 4, 2
    share = x.shape[0] // parts
    number = jnp.arange(n_tiles, dtype=jnp.int32)[:, None]
    ready = [(target[None, n * share:(n + 1) * share] == number).astype(jnp.bfloat16) for n in range(own, parts)]
    vmem = pl.BlockSpec(memory_space=pltpu.VMEM)
    return pl.pallas_call(
        sum_kernel,
        in_specs=[pl.BlockSpec(memory_space=pltpu.HBM)] + [vmem] * (2 + len(ready)),
        out_specs=vmem,
        out_shape=jax.ShapeDtypeStruct((n_tiles * chunk // LANES, LANES), jnp.bfloat16),
        scratch_shapes=[
            pltpu.VMEM(x.shape, x.dtype),
            pltpu.VMEM((n_tiles * chunk // LANES + 8, LANES), jnp.float32),
            pltpu.SemaphoreType.DMA((parts,)),
        ],
        compiler_params=pltpu.CompilerParams(vmem_limit_bytes=24 << 20),
    )(x, target.reshape(1, -1), update, *ready)


def final_kernel(n_down, n_across, x_ref, out_ref, spread_ref):
    held, tile, _ = out_ref.shape
    rows, cols = tile // n_down, tile // n_across
    per = LANES // cols
    quads = rows // per
    sides = tile // LANES
    for i in range(n_down):
        for h in range(sides):
            parts = [x_ref[device_of(i, h * per + j, n_across)].astype(jnp.float32) for j in range(per)]
            for r in range(per):
                picked = pick_lanes(parts, r, per)
                if r:
                    picked = pltpu.roll(picked, LANES - cols * r, axis=1)
                for s in range(held):
                    spread_ref[h, pl.ds(s * tile + i * rows + r, quads, stride=per), :] = (
                        picked[s * quads:(s + 1) * quads]
                    )
    for s in range(held):
        for h in range(sides):
            out_ref[s, :, h * LANES:(h + 1) * LANES] = spread_ref[h, s * tile:(s + 1) * tile, :]


def final_tiles(x, tile, held, n_down, n_across):
    vmem = pl.BlockSpec(memory_space=pltpu.VMEM)
    return pl.pallas_call(
        functools.partial(final_kernel, n_down, n_across),
        in_specs=[vmem],
        out_specs=vmem,
        out_shape=jax.ShapeDtypeStruct((held, tile, tile), jnp.float32),
        scratch_shapes=[pltpu.VMEM((tile // LANES, held * tile + 8, LANES), jnp.float32)],
        compiler_params=VMEM,
    )(x)


def per_device(a_tiles, scaling, dest_owner, dest_slot, panel, front_tiles):
    contribs, _, _, tile, _ = a_tiles.shape
    n_group, n_chip, n_core = (lax.axis_size(name) for name in AXES)
    n_dev = n_chip * n_core
    n_all = n_dev * n_group
    held = front_tiles.shape[0]
    n_tiles = n_all * held
    n_across = 8
    n_down = n_all // n_across
    rows, cols = tile // n_down, tile // n_across
    chunk = rows * cols
    depth = panel.shape[1]

    early = exchange(early_blocks(dest_owner[:, 0], dest_slot, front_tiles, panel, n_down, n_across), PLANE)
    arrived = exchange(form_products(a_tiles, scaling, n_down, n_across), AXES)

    even = lax.axis_index("core") == 0
    low, high, rest = early[:, :rows], early[:, rows:2 * rows], early[:, 2 * rows:]
    own = jnp.concatenate([jnp.where(even, low, high), rest], axis=1)
    other = jnp.concatenate([jnp.where(even, high, low), rest], axis=1)
    other = lax.ppermute(other, "core", [(0, 1), (1, 0)])
    early = jnp.where(even, jnp.stack([own, other], axis=1), jnp.stack([other, own], axis=1))
    early = early.reshape(n_group, n_dev, -1, depth)

    numbers = early[:, :, rows + cols].astype(jnp.int32).reshape(n_all, depth)
    owner, slot = numbers[:, :contribs].reshape(-1), numbers[:, contribs:2 * contribs].reshape(-1)
    target = (slot // held) * (n_dev * held) + owner * held + slot % held
    first = 2 * contribs
    row_piece = numbers[:, first:first + held].reshape(-1)
    col_piece = numbers[:, first + held:first + 2 * held].reshape(-1)

    per = LANES // cols
    chip = lax.axis_index("group") * n_chip + lax.axis_index("chip")
    left = early[:, :, :rows].reshape(n_group, n_dev, rows // per, per, depth)
    left = jnp.roll(left, chip % per, axis=3).reshape(n_group, n_dev, rows, depth)
    grid = jnp.einsum(
        "glrp,gsmp->lsrm", left, early[:, :, rows:rows + cols], preferred_element_type=jnp.float32
    ).reshape(n_dev * n_dev, chunk)
    update = jnp.take(grid, row_piece * n_dev + col_piece, axis=0, mode="clip")

    sums = sum_by_target(arrived.reshape(n_all * contribs, chunk), target, update)
    final = exchange(sums.reshape(n_all, held * chunk // LANES, LANES), AXES)
    return final_tiles(final, tile, held, n_down, n_across)


def solution(mesh):
    n_group, n_dev = mesh.devices.shape
    mesh = jax.sharding.Mesh(mesh.devices.reshape(n_group, n_dev // 2, 2), AXES)
    in_specs = (
        P(AXES, None, None, None, None),
        P(AXES, None, None),
        P(AXES, None),
        P(AXES),
        P(("chip", "core"), "group"),
        P(AXES, None),
    )
    out_specs = P(AXES, None, None)
    return jax.shard_map(
        per_device, mesh=mesh, in_specs=in_specs, out_specs=out_specs, check_vma=False
    )
```

```python
import functools
import jax
import jax.numpy as jnp
from jax import lax
from jax.experimental import pallas as pl
from jax.experimental.pallas import tpu as pltpu
from jax.sharding import PartitionSpec as P

AXES = ("group", "chip", "core")
PLANE = ("group", "chip")
LANES = 128
BATCH = 16
VMEM = pltpu.CompilerParams(vmem_limit_bytes=48 << 20)


def exchange(x, axes):
    return lax.all_to_all(x, axes, split_axis=0, concat_axis=0, tiled=True)


def device_of(i, j, n_across):
    return (i // 2) * (2 * n_across) + 2 * j + i % 2


def pick_lanes(parts, shift, per):
    group = lax.broadcasted_iota(jnp.int32, parts[0].shape, 1) // (LANES // per)
    result = parts[0]
    for n in range(1, per):
        result = jnp.where(group == (shift + n) % per, parts[n], result)
    return result


def early_kernel(n_down, n_across, owner_hbm, slot_hbm, front_hbm, panel_hbm, out_ref,
                 owner_ref, slot_ref, front_ref, panel_ref, sem_ref):
    pairs = [(owner_hbm, owner_ref), (slot_hbm, slot_ref), (front_hbm, front_ref), (panel_hbm, panel_ref)]
    copies = [pltpu.make_async_copy(a, b, sem_ref.at[n]) for n, (a, b) in enumerate(pairs)]
    for copy in copies:
        copy.start()
    for copy in copies:
        copy.wait()
    tile, depth = panel_ref.shape
    rows = tile // n_down
    count = owner_ref.shape[0]
    held = front_ref.shape[1]
    lane = lax.broadcasted_iota(jnp.int32, (8, depth), 1)
    numbers = jnp.zeros((8, depth), jnp.int32)
    for c in range(count):
        numbers = jnp.where(lane == c, owner_ref[c], numbers)
        numbers = jnp.where(lane == count + c, slot_ref[c], numbers)
    for s in range(held):
        for side in range(2):
            numbers = jnp.where(lane == 2 * count + side * held + s, front_ref[side, s], numbers)
    numbers = numbers.astype(jnp.float32).astype(jnp.bfloat16)
    cols = tile // n_across
    for a in range(n_down // 2):
        for j in range(n_across):
            chip = a * n_across + j
            out_ref[chip, 0:2 * rows, :] = panel_ref[2 * a * rows:2 * (a + 1) * rows, :]
            out_ref[chip, 2 * rows:2 * rows + cols, :] = panel_ref[j * cols:(j + 1) * cols, :]
            out_ref[chip, 2 * rows + cols:2 * rows + cols + 8, :] = numbers


def early_blocks(owner, slot, front_tiles, panel, n_down, n_across):
    tile, depth = panel.shape
    height = 2 * (tile // n_down) + tile // n_across + 8
    front = front_tiles.T
    hbm = pl.BlockSpec(memory_space=pltpu.HBM)
    return pl.pallas_call(
        functools.partial(early_kernel, n_down, n_across),
        in_specs=[hbm] * 4,
        out_specs=pl.BlockSpec(memory_space=pltpu.VMEM),
        out_shape=jax.ShapeDtypeStruct((n_down * n_across // 2, height, depth), jnp.bfloat16),
        scratch_shapes=[
            pltpu.SMEM(owner.shape, owner.dtype),
            pltpu.SMEM(slot.shape, slot.dtype),
            pltpu.SMEM(front.shape, front.dtype),
            pltpu.VMEM(panel.shape, panel.dtype),
            pltpu.SemaphoreType.DMA((4,)),
        ],
        compiler_params=pltpu.CompilerParams(vmem_limit_bytes=64 << 20),
    )(owner, slot, front, panel)


def products_kernel(n_down, n_across, a_ref, scale_ref, out_ref, held_ref):
    count, blocks, _, tile, _ = a_ref.shape
    rows, cols = tile // n_down, tile // n_across
    per = LANES // cols
    quads = rows // per
    sides = tile // LANES
    step = pl.program_id(1)
    for u in range(count):
        total = None
        for k in range(blocks):
            scaled = (a_ref[u, k, 0].astype(jnp.float32) * scale_ref[u, k][None, :]).astype(jnp.bfloat16)
            part = lax.dot_general(
                scaled, a_ref[u, k, 1], (((1,), (1,)), ((), ())), preferred_element_type=jnp.float32
            )
            total = part if total is None else total + part
        for h in range(sides):
            held_ref[h, pl.ds(step * count + u, tile, stride=BATCH), :] = total[:, h * LANES:(h + 1) * LANES]

    @pl.when(step == pl.num_programs(1) - 1)
    def _():
        @pl.loop(0, n_down // 2)
        def _(pair):
            for d in range(2):
                for q in range(quads):
                    for h in range(sides):
                        parts = []
                        for r in range(per):
                            row = ((pair * 2 + d) * rows + q * per + r) * BATCH
                            part = held_ref[h, pl.ds(pl.multiple_of(row, BATCH), BATCH), :]
                            parts.append(pltpu.roll(part, cols * r, axis=1) if r else part)
                        for j in range(per):
                            first = pair * (2 * n_across) + device_of(d, h * per + j, n_across)
                            out_ref[first, :, q * LANES:(q + 1) * LANES] = pick_lanes(parts, j, per).astype(jnp.bfloat16)


def form_products(a_tiles, scaling, n_down, n_across):
    contribs, blocks, _, tile, _ = a_tiles.shape
    n_all = n_down * n_across
    chunk = tile * tile // n_all
    count = 8
    steps = BATCH // count
    return pl.pallas_call(
        functools.partial(products_kernel, n_down, n_across),
        grid=(contribs // BATCH, steps),
        in_specs=[
            pl.BlockSpec((count, blocks, 2, tile, tile), lambda g, s: (g * steps + s, 0, 0, 0, 0)),
            pl.BlockSpec((count, blocks, tile), lambda g, s: (g * steps + s, 0, 0)),
        ],
        out_specs=pl.BlockSpec((n_all, BATCH, chunk), lambda g, s: (0, g, 0)),
        out_shape=jax.ShapeDtypeStruct((n_all, contribs, chunk), jnp.bfloat16),
        scratch_shapes=[pltpu.VMEM((tile // LANES, (tile + 1) * BATCH, LANES), jnp.float32)],
        compiler_params=pltpu.CompilerParams(vmem_limit_bytes=64 << 20),
    )(a_tiles, scaling)


def sum_kernel(x_hbm, target_ref, update_ref, *refs):
    ready_refs, (out_ref, x_ref, spread_ref, sem_ref) = refs[:-4], refs[-4:]
    n_tiles, chunk = update_ref.shape
    parts = sem_ref.shape[0]
    share = x_ref.shape[0] // parts
    own = parts - len(ready_refs)
    copies = []
    for n in range(parts):
        at = pl.ds(n * share, share)
        copies.append(pltpu.make_async_copy(x_hbm.at[at], x_ref.at[at], sem_ref.at[n]))
        copies[n].start()
    number = lax.broadcasted_iota(jnp.int32, (n_tiles, share), 0)
    total = -update_ref[...]
    for n in range(parts):
        at = slice(n * share, (n + 1) * share)
        if n < own:
            picking = jnp.where(number == target_ref[:, at], 1.0, 0.0).astype(jnp.bfloat16)
        else:
            picking = ready_refs[n - own][...]
        copies[n].wait()
        total += jnp.dot(picking, x_ref[at, :], preferred_element_type=jnp.float32)
    pieces = chunk // LANES
    for q in range(pieces):
        spread_ref[pl.ds(q, n_tiles, stride=pieces), :] = total[:, q * LANES:(q + 1) * LANES]
    out_ref[...] = spread_ref[0:n_tiles * pieces, :].astype(jnp.bfloat16)


def sum_by_target(x, target, update):
    n_tiles, chunk = update.shape
    parts, own = 4, 1
    share = x.shape[0] // parts
    number = jnp.arange(n_tiles, dtype=jnp.int32)[:, None]
    ready = [(target[None, n * share:(n + 1) * share] == number).astype(jnp.bfloat16) for n in range(own, parts)]
    vmem = pl.BlockSpec(memory_space=pltpu.VMEM)
    return pl.pallas_call(
        sum_kernel,
        in_specs=[pl.BlockSpec(memory_space=pltpu.HBM)] + [vmem] * (2 + len(ready)),
        out_specs=vmem,
        out_shape=jax.ShapeDtypeStruct((n_tiles * chunk // LANES, LANES), jnp.bfloat16),
        scratch_shapes=[
            pltpu.VMEM(x.shape, x.dtype),
            pltpu.VMEM((n_tiles * chunk // LANES + 8, LANES), jnp.float32),
            pltpu.SemaphoreType.DMA((parts,)),
        ],
        compiler_params=pltpu.CompilerParams(vmem_limit_bytes=12 << 20),
    )(x, target.reshape(1, -1), update, *ready)


def final_kernel(n_down, n_across, x_ref, out_ref, spread_ref):
    held, tile, _ = out_ref.shape
    rows, cols = tile // n_down, tile // n_across
    per = LANES // cols
    quads = rows // per
    sides = tile // LANES
    for i in range(n_down):
        for h in range(sides):
            parts = [x_ref[device_of(i, h * per + j, n_across)].astype(jnp.float32) for j in range(per)]
            for r in range(per):
                picked = pick_lanes(parts, r, per)
                if r:
                    picked = pltpu.roll(picked, LANES - cols * r, axis=1)
                for s in range(held):
                    spread_ref[h, pl.ds(s * tile + i * rows + r, quads, stride=per), :] = (
                        picked[s * quads:(s + 1) * quads]
                    )
    for s in range(held):
        for h in range(sides):
            out_ref[s, :, h * LANES:(h + 1) * LANES] = spread_ref[h, s * tile:(s + 1) * tile, :]


def final_tiles(x, tile, held, n_down, n_across):
    vmem = pl.BlockSpec(memory_space=pltpu.VMEM)
    return pl.pallas_call(
        functools.partial(final_kernel, n_down, n_across),
        in_specs=[vmem],
        out_specs=vmem,
        out_shape=jax.ShapeDtypeStruct((held, tile, tile), jnp.float32),
        scratch_shapes=[pltpu.VMEM((tile // LANES, held * tile + 8, LANES), jnp.float32)],
        compiler_params=VMEM,
    )(x)


def per_device(a_tiles, scaling, dest_owner, dest_slot, panel, front_tiles):
    contribs, _, _, tile, _ = a_tiles.shape
    n_group, n_chip, n_core = (lax.axis_size(name) for name in AXES)
    n_dev = n_chip * n_core
    n_all = n_dev * n_group
    held = front_tiles.shape[0]
    n_tiles = n_all * held
    n_across = 8
    n_down = n_all // n_across
    rows, cols = tile // n_down, tile // n_across
    chunk = rows * cols
    depth = panel.shape[1]

    early = exchange(early_blocks(dest_owner[:, 0], dest_slot, front_tiles, panel, n_down, n_across), PLANE)
    arrived = exchange(form_products(a_tiles, scaling, n_down, n_across), AXES)

    even = lax.axis_index("core") == 0
    low, high, rest = early[:, :rows], early[:, rows:2 * rows], early[:, 2 * rows:]
    own = jnp.concatenate([jnp.where(even, low, high), rest], axis=1)
    other = jnp.concatenate([jnp.where(even, high, low), rest], axis=1)
    other = lax.ppermute(other, "core", [(0, 1), (1, 0)])
    early = jnp.where(even, jnp.stack([own, other], axis=1), jnp.stack([other, own], axis=1))
    early = early.reshape(n_group, n_dev, -1, depth)

    numbers = early[:, :, rows + cols].astype(jnp.int32).reshape(n_all, depth)
    owner, slot = numbers[:, :contribs].reshape(-1), numbers[:, contribs:2 * contribs].reshape(-1)
    target = (slot // held) * (n_dev * held) + owner * held + slot % held
    first = 2 * contribs
    row_piece = numbers[:, first:first + held].reshape(-1)
    col_piece = numbers[:, first + held:first + 2 * held].reshape(-1)

    per = LANES // cols
    chip = lax.axis_index("group") * n_chip + lax.axis_index("chip")
    left = early[:, :, :rows].reshape(n_group, n_dev, rows // per, per, depth)
    left = jnp.roll(left, chip % per, axis=3).reshape(n_group, n_dev, rows, depth)
    grid = jnp.einsum(
        "glrp,gsmp->lsrm", left, early[:, :, rows:rows + cols], preferred_element_type=jnp.float32
    ).reshape(n_dev * n_dev, chunk)
    update = jnp.take(grid, row_piece * n_dev + col_piece, axis=0, mode="clip")

    sums = sum_by_target(arrived.reshape(n_all * contribs, chunk), target, update)
    final = exchange(sums.reshape(n_all, held * chunk // LANES, LANES), AXES)
    return final_tiles(final, tile, held, n_down, n_across)


def solution(mesh):
    n_group, n_dev = mesh.devices.shape
    mesh = jax.sharding.Mesh(mesh.devices.reshape(n_group, n_dev // 2, 2), AXES)
    in_specs = (
        P(AXES, None, None, None, None),
        P(AXES, None, None),
        P(AXES, None),
        P(AXES),
        P(("chip", "core"), "group"),
        P(AXES, None),
    )
    out_specs = P(AXES, None, None)
    return jax.shard_map(
        per_device, mesh=mesh, in_specs=in_specs, out_specs=out_specs, check_vma=False
    )
```
